32 devices in a mesh: row: 8 (over z, core), col: 4 (over y, x).
Axes of the slice: x: 2, y: 2, z: 4, core: 2. Of those that a mesh axis runs over, the one named last changes fastest.
Arguments:
- packed_tiles: bfloat16 [384, 128, 512], P('row', None, 'col'), may hold values from -6 to 6
- source_pick: int32 [8, 48], P('row'), may hold values from 0 to 47, each once within a row
- owner_place: int32 [8, 48], P('row'), may hold values from 0 to 47, each once within a row
- tile_orient: int32 [8, 48], P('row'), may hold values from 0 to 3
- w_panel: bfloat16 [2048, 6144], P('row', 'col'), may hold values from -0.125 to 0.125
Outputs:
- particle_hole: bfloat16 [12288, 6144], P('row', 'col')
The draws below stay inside these ranges and needn't reach their ends.
Inputs may be any that keep to these rules, and one draw needn't show every extreme that they name: `source_pick`: each row is a permutation of the stored tiles' local indices. `owner_place`: each row is a permutation of the received items.
All inputs are finite; a program needn't handle non-finite values.
Results may differ from the reference program's by a relative error of at most 0.001.
Values may be sent and summed in bfloat16 or wider, within the bound.
A program may use at most 128 MiB of HBM per device.

```python
import jax
import jax.numpy as jnp

TILE = 128
VW = 768
KC = 512
STORED = 48
ROWS = 12288
COLS = 6144
K = 2048
N_ROW = 8
N_COL = 4


def with_ends(values, key, low, top_value):
    place = [jax.random.randint(jax.random.fold_in(key, axis), (), 0, length) for axis, length in enumerate(values.shape)]
    main_axis = values.shape.index(max(values.shape))
    beside = place[:main_axis] + [(place[main_axis] + 1) % values.shape[main_axis]] + place[main_axis + 1:]
    return values.at[tuple(place)].set(low).at[tuple(beside)].set(top_value)


def level_of(rng, shape, split, smallest, largest):
    def one(dim, shards_of):
        heights = jax.random.uniform(jax.random.fold_in(jax.random.fold_in(rng, 6), dim), (shards_of,), jnp.float32, smallest / len(split), largest / len(split))
        return jnp.repeat(jnp.exp(heights), shape[dim] // shards_of).reshape((-1,) + (1,) * (len(shape) - dim - 1))

    gain = one(*split[0])
    for cut in split[1:]:
        gain = gain * one(*cut)
    return gain


def gaussian(key, extent, spread, limit, shards=(), held_as=jnp.bfloat16):
    entries = jax.random.normal(key, extent, jnp.float32) * spread
    if len(shards) > 0:
        entries = level_of(key, extent, shards, -0.22, 0.18) * entries
    return jnp.clip(entries, min=-limit, max=limit).astype(held_as)


def setup_inputs(seed: int = 0) -> dict:
    splits = jax.random.split(jax.random.key(seed), 6)
    return {
        "packed_tiles": gaussian(splits[0], (N_ROW * STORED, TILE, N_COL * TILE), 1.0, 6.0, ((0, 8), (2, 4))),
        "source_pick": jax.vmap(lambda own: jax.random.permutation(own, STORED))(jax.random.split(splits[1], N_ROW)).reshape((N_ROW, STORED)).astype(jnp.int32),
        "owner_place": jax.vmap(lambda own: jax.random.permutation(own, STORED))(jax.random.split(splits[2], N_ROW)).reshape((N_ROW, STORED)).astype(jnp.int32),
        "tile_orient": with_ends(jax.random.randint(splits[3], (N_ROW, STORED), 0, 4), jax.random.fold_in(splits[3], 1), 0, 3).astype(jnp.int32),
        "w_panel": gaussian(splits[4], (K, COLS), K ** -0.5, 0.125, ((0, 8), (1, 4))),
    }


def reference(packed_tiles, source_pick, owner_place, tile_orient, w_panel):
    peer_slots = STORED // N_ROW
    target = jnp.arange(N_ROW, dtype=jnp.int32)[:, None]
    source = owner_place // peer_slots
    slot_index = owner_place % peer_slots
    local_index = source_pick[source, target * peer_slots + slot_index]
    flat_index = (source * STORED + local_index).reshape(-1).astype(jnp.int32)
    tile_set = packed_tiles[flat_index].reshape(N_ROW * STORED, TILE, N_COL, TILE)
    orient_codes = tile_orient.reshape(-1)
    flipped = (orient_codes % 2 == 1)[:, None, None, None]
    negated = (orient_codes >= 2)[:, None, None, None]
    turned = jnp.where(flipped, jnp.swapaxes(tile_set, 1, 3), tile_set)
    turned = jnp.where(negated, -turned, turned)
    col_tiles = KC // TILE
    row_tiles = STORED // col_tiles
    lambda_rows = turned.reshape(N_ROW, row_tiles, col_tiles, TILE, N_COL, TILE)
    lambda_rows = lambda_rows.transpose(0, 1, 3, 4, 2, 5).reshape(ROWS, K)
    product = jnp.dot(lambda_rows, w_panel, preferred_element_type=jnp.float32)
    blocked = product.reshape(ROWS // VW, VW, COLS // VW, VW)
    return (blocked - blocked.transpose(0, 3, 2, 1)).reshape(ROWS, COLS).astype(jnp.bfloat16)
```

```python
import functools

import jax
import jax.numpy as jnp
from jax import lax
from jax.experimental import pallas as pl
from jax.experimental.pallas import tpu as pltpu
from jax.sharding import PartitionSpec as P

VW = 768
MESH = pl.DeviceIdType.MESH


def kernel(
    n_row, n_col, tiles_hbm, pick, place, orient, w_hbm, out_hbm,
    tiles, outgoing, incoming, lam, panel, prod, result,
    load_sem, out_sem, a_send, a_recv, p_send, p_recv, l_send, l_fwd, l_recv,
):
    row, col = lax.axis_index("row"), lax.axis_index("col")
    chip, core = row // 2, row % 2
    chips = n_row // 2
    sibling = chip * 2 + 1 - core
    wide = 2
    high = n_col // wide
    hi, lo = col // wide, col % wide

    stored, tw, _ = tiles.shape
    slots = stored // n_row
    depth = panel.shape[0] // n_row
    height, kc = lam.shape[1], lam.shape[2]
    half = height // 2
    v_tiles = kc // tw
    breadth = panel.shape[1]

    load_tiles = pltpu.make_async_copy(tiles_hbm, tiles, load_sem.at[0])
    load_tiles.start()
    own_rows = pl.ds(pl.multiple_of(row * depth, depth), depth)
    load_w = pltpu.make_async_copy(w_hbm, panel.at[own_rows], load_sem.at[1])
    load_w.start()

    def row_peer(p):
        return lax.rem(row + p, n_row)

    x_peers = [hi * wide + lax.rem(lo + p, wide) for p in range(1, wide)]
    y_peers = [lax.rem(hi + p, high) * wide + lo for p in range(1, high)]

    barrier = pltpu.get_barrier_semaphore()
    for p in range(1, n_row):
        pl.semaphore_signal(barrier, inc=1, device_id=(row_peer(p), col), device_id_type=MESH)
    for c in x_peers + y_peers:
        pl.semaphore_signal(barrier, inc=1, device_id=(row, c), device_id_type=MESH)

    load_tiles.wait()

    def choose(t, carry):
        outgoing[t] = tiles[pick[0, t]]
        return carry

    lax.fori_loop(0, stored, choose, 0)
    load_w.wait()
    pl.semaphore_wait(barrier, n_row - 1 + len(x_peers) + len(y_peers))

    def exchange(p):
        to = row_peer(p)
        return pltpu.make_async_remote_copy(
            src_ref=outgoing.at[pl.ds(to * slots, slots)],
            dst_ref=incoming.at[pl.ds(row * slots, slots)],
            send_sem=a_send.at[p],
            recv_sem=a_recv.at[p],
            device_id=(to, col),
            device_id_type=MESH,
        )

    for p in range(1, n_row):
        exchange(p).start()

    def pass_on(slot, way, to):
        rows = pl.ds(pl.multiple_of(slot * depth, depth), depth)
        return pltpu.make_async_remote_copy(
            src_ref=panel.at[rows],
            dst_ref=panel.at[rows],
            send_sem=p_send.at[slot, way],
            recv_sem=p_recv.at[slot],
            device_id=(to, col),
            device_id_type=MESH,
        )

    has_left, has_right = chip > 0, chip < chips - 1

    pass_on(row, 2, sibling).start()

    def keep(t, carry):
        incoming[row * slots + t] = outgoing[row * slots + t]
        return carry

    lax.fori_loop(0, slots, keep, 0)
    for p in range(1, n_row):
        exchange(p).wait()

    @pl.when(has_left)
    def _():
        pass_on(row, 0, row - 2).start()

    @pl.when(has_right)
    def _():
        pass_on(row, 1, row + 2).start()

    def assemble(u, carry):
        for v in range(v_tiles):
            o = u * v_tiles + v
            code = orient[0, o]
            tile = incoming[place[0, o]].astype(jnp.float32)
            turned = jnp.where(code % 2 == 1, tile.T, tile)
            turned = jnp.where(code >= 2, -turned, turned)
            lam[col, pl.ds(pl.multiple_of(u * tw, tw), tw), v * tw:(v + 1) * tw] = turned.astype(jnp.bfloat16)
        return carry

    lax.fori_loop(0, stored // v_tiles, assemble, 0)

    def spread(block, h, sem, to):
        part = lam.at[block, h * half:(h + 1) * half]
        return pltpu.make_async_remote_copy(
            src_ref=part,
            dst_ref=part,
            send_sem=sem,
            recv_sem=l_recv.at[block, h],
            device_id=(row, to),
            device_id_type=MESH,
        )

    sent = []
    for first in range(2):
        for n, c in enumerate(x_peers):
            sent.append(spread(col, first, l_send.at[n, first], c))
            sent[-1].start()
        for n, c in enumerate(y_peers):
            sent.append(spread(col, 1 - first, l_send.at[wide - 1 + n, 1 - first], c))
            sent[-1].start()

    def panel_step(t):
        @pl.when(chip >= t)
        def _():
            slot = row - 2 * t
            pass_on(slot, 1, row).wait_recv()

            @pl.when(has_right)
            def _():
                pass_on(slot, 1, row + 2).start()

            pass_on(slot, 2, sibling).start()

        @pl.when(chip + t < chips)
        def _():
            slot = row + 2 * t
            pass_on(slot, 0, row).wait_recv()

            @pl.when(has_left)
            def _():
                pass_on(slot, 0, row - 2).start()

            pass_on(slot, 2, sibling).start()

    panel_step(1)
    for n, c in enumerate(x_peers):
        spread(c, 0, l_send.at[0, 0], col).wait_recv()
        for m, d in enumerate(y_peers):
            sent.append(spread(c, 0, l_fwd.at[0, n, m], d))
            sent[-1].start()
    for m, c in enumerate(y_peers):
        spread(c, 1, l_send.at[0, 0], col).wait_recv()
        for n, d in enumerate(x_peers):
            sent.append(spread(c, 1, l_fwd.at[1, n, m], d))
            sent[-1].start()
    for t in range(2, chips):
        panel_step(t)
    for q in range(chips):
        pass_on(q * 2 + 1 - core, 2, sibling).wait_recv()
    for c in x_peers:
        spread(c, 1, l_send.at[0, 0], col).wait_recv()
    for c in y_peers:
        spread(c, 0, l_send.at[0, 0], col).wait_recv()
    for n in range(1, wide):
        for m in range(1, high):
            diag = lax.rem(hi + m, high) * wide + lax.rem(lo + n, wide)
            for h in range(2):
                spread(diag, h, l_send.at[0, 0], col).wait_recv()

    pairs_i, pairs_j = height // VW, breadth // VW
    strip = VW // 3

    def block_out(i, j):
        return pltpu.make_async_copy(
            result.at[pl.ds(pl.multiple_of(i * VW, VW), VW), pl.ds(pl.multiple_of(j * VW, VW), VW)],
            out_hbm.at[pl.ds(pl.multiple_of(i * VW, VW), VW), pl.ds(pl.multiple_of(j * VW, VW), VW)],
            out_sem.at[i * pairs_j + j],
        )

    def one(ij, carry):
        i, j = ij // pairs_j, ij % pairs_j
        across = pl.ds(pl.multiple_of(j * VW, VW), VW)
        for a in range(3):
            down = pl.ds(pl.multiple_of(i * VW + a * strip, strip), strip)
            total = None
            for g in range(n_col):
                term = jnp.dot(
                    lam[g, down, :], panel[g * kc:(g + 1) * kc, across],
                    preferred_element_type=jnp.float32,
                )
                total = term if total is None else total + term
            prod[a * strip:(a + 1) * strip, :] = total
        for a in range(3):
            down = pl.ds(pl.multiple_of(i * VW + a * strip, strip), strip)
            mirrored = prod[:, a * strip:(a + 1) * strip].T
            result[down, across] = (prod[a * strip:(a + 1) * strip, :] - mirrored).astype(jnp.bfloat16)
        block_out(i, j).start()
        return carry

    lax.fori_loop(0, pairs_i * pairs_j, one, 0)

    for copy in sent:
        copy.wait_send()
    pass_on(row, 2, sibling).wait_send()

    @pl.when(has_left)
    def _():
        pass_on(row, 0, row - 2).wait_send()

    @pl.when(has_right)
    def _():
        pass_on(row, 1, row + 2).wait_send()

    for t in range(1, chips):
        @pl.when(chip >= t)
        def _(t=t):
            @pl.when(has_right)
            def _():
                pass_on(row - 2 * t, 1, row + 2).wait_send()

            pass_on(row - 2 * t, 2, sibling).wait_send()

        @pl.when(chip + t < chips)
        def _(t=t):
            @pl.when(has_left)
            def _():
                pass_on(row + 2 * t, 0, row - 2).wait_send()

            pass_on(row + 2 * t, 2, sibling).wait_send()

    for i in range(pairs_i):
        for j in range(pairs_j):
            block_out(i, j).wait()


def on_device(n_row, n_col, packed_tiles, source_pick, owner_place, tile_orient, w_panel):
    stored, tw, _ = packed_tiles.shape
    depth, breadth = w_panel.shape
    k = depth * n_row
    kc = k // n_col
    height = stored // (kc // tw) * tw
    wide = 2
    high = n_col // wide
    dma = pltpu.SemaphoreType.DMA
    smem = pl.BlockSpec(memory_space=pltpu.SMEM)
    anywhere = pl.BlockSpec(memory_space=pl.ANY)
    return pl.pallas_call(
        functools.partial(kernel, n_row, n_col),
        out_shape=jax.ShapeDtypeStruct((height, breadth), jnp.bfloat16),
        in_specs=[anywhere, smem, smem, smem, anywhere],
        out_specs=anywhere,
        scratch_shapes=[
            pltpu.VMEM((stored, tw, tw), jnp.bfloat16),
            pltpu.VMEM((stored, tw, tw), jnp.bfloat16),
            pltpu.VMEM((stored, tw, tw), jnp.bfloat16),
            pltpu.VMEM((n_col, height, kc), jnp.bfloat16),
            pltpu.VMEM((k, breadth), jnp.bfloat16),
            pltpu.VMEM((VW, VW), jnp.float32),
            pltpu.VMEM((height, breadth), jnp.bfloat16),
            dma((2,)),
            dma(((height // VW) * (breadth // VW),)),
            dma((n_row,)),
            dma((n_row,)),
            dma((n_row, 3)),
            dma((n_row,)),
            dma((wide + high - 2, 2)),
            dma((2, wide - 1, high - 1)),
            dma((n_col, 2)),
        ],
        compiler_params=pltpu.CompilerParams(
            collective_id=0, has_side_effects=True, vmem_limit_bytes=56 * 2**20
        ),
        cost_estimate=pl.CostEstimate(
            flops=2 * height * breadth * k, bytes_accessed=4 * height * breadth, transcendentals=0
        ),
    )(packed_tiles, source_pick, owner_place, tile_orient, w_panel)


def solution(mesh):
    in_specs = (
        P("row", None, "col"),
        P("row", None),
        P("row", None),
        P("row", None),
        P("row", "col"),
    )
    return jax.shard_map(
        functools.partial(on_device, mesh.shape["row"], mesh.shape["col"]),
        mesh=mesh, in_specs=in_specs, out_specs=P("row", "col"), check_vma=False,
    )
```

```python
import functools

import jax
import jax.numpy as jnp
from jax import lax
from jax.experimental import pallas as pl
from jax.experimental.pallas import tpu as pltpu
from jax.sharding import PartitionSpec as P

VW = 768
PIECES = 4
MESH = pl.DeviceIdType.MESH


def kernel(
    n_row, n_col, tiles_hbm, pick, place, orient, w_hbm, prod,
    tiles, outgoing, raw, lam, panel,
    load_sem, a_send, p_send, p_recv, l_send, l_fwd, l_recv,
):
    row, col = lax.axis_index("row"), lax.axis_index("col")
    chip, core = row // 2, row % 2
    chips = n_row // 2
    sibling = chip * 2 + 1 - core
    wide = 2
    high = n_col // wide
    hi, lo = col // wide, col % wide

    stored, tw, _ = tiles.shape
    slots = stored // n_row
    depth = panel.shape[0] // n_row
    height, kc = lam.shape[1], lam.shape[2]
    v_tiles = kc // tw
    breadth = panel.shape[1]
    piece = depth // PIECES

    load_tiles = pltpu.make_async_copy(tiles_hbm, tiles, load_sem.at[0])
    load_tiles.start()
    own_rows = pl.ds(pl.multiple_of(row * depth, depth), depth)
    load_w = pltpu.make_async_copy(w_hbm, panel.at[own_rows], load_sem.at[1])
    load_w.start()

    def row_peer(p):
        return lax.rem(row + p, n_row)

    own = (0, 0)
    x_peers = [(0, p) for p in range(1, wide)]
    y_peers = [(p, 0) for p in range(1, high)]
    diagonals = [(m, n) for n in range(1, wide) for m in range(1, high)]

    def col_of(at):
        return lax.rem(hi + at[0], high) * wide + lax.rem(lo + at[1], wide)

    def number(at):
        return at[0] * wide + at[1]

    barrier = pltpu.get_barrier_semaphore()
    for p in range(1, n_row):
        pl.semaphore_signal(barrier, inc=1, device_id=(row_peer(p), col), device_id_type=MESH)
    for c in x_peers + y_peers:
        pl.semaphore_signal(barrier, inc=1, device_id=(row, col_of(c)), device_id_type=MESH)

    load_tiles.wait()

    def choose(t, carry):
        outgoing[t] = tiles[pick[0, t]]
        return carry

    lax.fori_loop(0, stored, choose, 0)
    pl.semaphore_wait(barrier, n_row - 1 + len(x_peers) + len(y_peers))

    def exchange(p):
        to = row_peer(p)
        return pltpu.make_async_remote_copy(
            src_ref=outgoing.at[pl.ds(to * slots, slots)],
            dst_ref=raw[0].at[pl.ds(row * slots, slots)],
            send_sem=a_send.at[p],
            recv_sem=l_recv.at[0, row],
            device_id=(to, col),
            device_id_type=MESH,
        )

    def pass_on(slot, r, way, to):
        rows = pl.ds(pl.multiple_of(slot * depth + r * piece, piece), piece)
        return pltpu.make_async_remote_copy(
            src_ref=panel.at[rows],
            dst_ref=panel.at[rows],
            send_sem=p_send.at[slot, r, way],
            recv_sem=p_recv.at[slot, r],
            device_id=(to, col),
            device_id_type=MESH,
        )

    def spread(block, s, sem, to):
        there = number(((block[0] - to[0]) % high, (block[1] - to[1]) % wide))
        items = pl.ds(s * slots, slots)
        return pltpu.make_async_remote_copy(
            src_ref=raw[number(block)].at[items],
            dst_ref=raw[there].at[items],
            send_sem=sem,
            recv_sem=l_recv.at[there, s],
            device_id=(row, col_of(to)),
            device_id_type=MESH,
        )

    def arrived(block, s):
        spread(block, s, l_send.at[s, 0], own).wait_recv()

    has_left, has_right = chip > 0, chip < chips - 1

    def to_sides(act):
        for r in range(PIECES):
            @pl.when(has_left)
            def _(r=r):
                act(pass_on(row, r, 0, row - 2))

            @pl.when(has_right)
            def _(r=r):
                act(pass_on(row, r, 1, row + 2))

    def chips_at(t, act):
        if t == 0:
            act(chip)
            return

        @pl.when(chip >= t)
        def _():
            act(chip - t)

        @pl.when(chip + t < chips)
        def _():
            act(chip + t)

    def direct(t):
        def act(q):
            for k in range(2):
                s = q * 2 + k
                arrived(own, s)
                for n, c in enumerate(x_peers + y_peers):
                    spread(own, s, l_send.at[s, n], c).start()

        chips_at(t, act)

    def onward(t):
        def act(q):
            for n, c in enumerate(x_peers):
                arrived(c, q * 2)
                for m, d in enumerate(y_peers):
                    spread(c, q * 2, l_fwd.at[q * 2, n, m], d).start()
            for m, c in enumerate(y_peers):
                arrived(c, q * 2 + 1)
                for n, d in enumerate(x_peers):
                    spread(c, q * 2 + 1, l_fwd.at[q * 2 + 1, n, m], d).start()

        chips_at(t, act)

    def panel_step(t, r):
        @pl.when(chip >= t)
        def _():
            slot = row - 2 * t
            pass_on(slot, r, 1, row).wait_recv()

            @pl.when(has_right)
            def _():
                pass_on(slot, r, 1, row + 2).start()

            pass_on(slot, r, 2, sibling).start()

        @pl.when(chip + t < chips)
        def _():
            slot = row + 2 * t
            pass_on(slot, r, 0, row).wait_recv()

            @pl.when(has_left)
            def _():
                pass_on(slot, r, 0, row - 2).start()

            pass_on(slot, r, 2, sibling).start()

    def rest_of_neighbours():
        for s in range(n_row):
            for c in x_peers if s % 2 else y_peers:
                arrived(c, s)

    def rest_of_diagonals():
        for c in diagonals:
            for s in range(n_row):
                arrived(c, s)

    def assemble(block):
        g, items = col_of(block), raw[number(block)]

        def one(u, carry):
            for v in range(v_tiles):
                o = u * v_tiles + v
                code = orient[0, o]
                tile = items[place[0, o]].astype(jnp.float32)
                turned = jnp.where(code % 2 == 1, tile.T, tile)
                turned = jnp.where(code >= 2, -turned, turned)
                lam[g, pl.ds(pl.multiple_of(u * tw, tw), tw), v * tw:(v + 1) * tw] = turned.astype(jnp.bfloat16)
            return carry

        lax.fori_loop(0, height // tw, one, 0)

    for p in range(1, n_row):
        exchange(p).start()
    load_w.wait()
    to_sides(lambda copy: copy.start())
    for r in range(PIECES):
        pass_on(row, r, 2, sibling).start()

    def keep(t, carry):
        raw[0][row * slots + t] = outgoing[row * slots + t]
        return carry

    lax.fori_loop(0, slots, keep, 0)
    for n, c in enumerate(x_peers + y_peers):
        spread(own, row, l_send.at[row, n], c).start()
    arrived(own, sibling)
    for n, c in enumerate(x_peers + y_peers):
        spread(own, sibling, l_send.at[sibling, n], c).start()
    for t in range(1, chips - 1):
        direct(t)
    panel_step(1, 0)
    direct(chips - 1)
    panel_step(1, 1)
    onward(0)
    for r in range(2, PIECES):
        panel_step(1, r)
        onward(r - 1)
    for t in range(PIECES - 1, chips - 1):
        onward(t)
    assemble(own)
    onward(chips - 1)
    steps = [(t, r) for t in range(2, chips - 1) for r in range(PIECES)]
    for t, r in steps[:-1]:
        panel_step(t, r)
    rest_of_neighbours()
    for c in x_peers + y_peers:
        assemble(c)
    panel_step(*steps[-1])
    rest_of_diagonals()
    for c in diagonals:
        assemble(c)

    strip = VW // 3
    across_n = breadth // VW

    def multiply(q, first):
        for r in range(PIECES):
            pass_on(q * 2 + 1 - core, r, 2, sibling).wait_recv()

        def one(step, carry):
            i, j = step // across_n, step % across_n
            down = pl.ds(pl.multiple_of(i * strip, strip), strip)
            across = pl.ds(pl.multiple_of(j * VW, VW), VW)
            term = jnp.dot(
                lam[q, down, :], panel[pl.ds(pl.multiple_of(q * kc, kc), kc), across],
                preferred_element_type=jnp.float32,
            )
            prod[down, across] = term if first else prod[down, across] + term
            return carry

        lax.fori_loop(0, height // strip * across_n, one, 0)

    multiply(chip, True)
    for t in range(1, chips):
        if t == chips - 1:
            for r in range(PIECES):
                panel_step(t, r)
        chips_at(t, functools.partial(multiply, first=False))

    for p in range(1, n_row):
        exchange(p).wait_send()
    for s in range(n_row):
        for n in range(wide + high - 2):
            spread(own, s, l_send.at[s, n], own).wait_send()
        for n in range(wide - 1):
            for m in range(high - 1):
                spread(own, s, l_fwd.at[s, n, m], own).wait_send()
    to_sides(lambda copy: copy.wait_send())
    for r in range(PIECES):
        pass_on(row, r, 2, sibling).wait_send()
        for t in range(1, chips):
            @pl.when(chip >= t)
            def _(t=t, r=r):
                @pl.when(has_right)
                def _():
                    pass_on(row - 2 * t, r, 1, row + 2).wait_send()

                pass_on(row - 2 * t, r, 2, sibling).wait_send()

            @pl.when(chip + t < chips)
            def _(t=t, r=r):
                @pl.when(has_left)
                def _():
                    pass_on(row + 2 * t, r, 0, row - 2).wait_send()

                pass_on(row + 2 * t, r, 2, sibling).wait_send()


def antisymmetrize(prod, out):
    strip = out.shape[0]
    i, j, a = pl.program_id(0), pl.program_id(1), pl.program_id(2)
    across = pl.ds(pl.multiple_of(j * VW, VW), VW)
    straight = prod[pl.ds(pl.multiple_of(i * VW + a * strip, strip), strip), across]
    crossed = prod[pl.ds(pl.multiple_of(i * VW, VW), VW), pl.ds(pl.multiple_of(j * VW + a * strip, strip), strip)]
    out[...] = (straight - crossed.T).astype(out.dtype)


def on_device(n_row, n_col, packed_tiles, source_pick, owner_place, tile_orient, w_panel):
    stored, tw, _ = packed_tiles.shape
    depth, breadth = w_panel.shape
    k = depth * n_row
    kc = k // n_col
    assert kc == 2 * depth
    height = stored // (kc // tw) * tw
    wide = 2
    high = n_col // wide
    dma = pltpu.SemaphoreType.DMA
    smem = pl.BlockSpec(memory_space=pltpu.SMEM)
    vmem = pl.BlockSpec(memory_space=pltpu.VMEM)
    anywhere = pl.BlockSpec(memory_space=pl.ANY)
    prod = pl.pallas_call(
        functools.partial(kernel, n_row, n_col),
        out_shape=pltpu.VMEM((height, breadth), jnp.float32),
        in_specs=[anywhere, smem, smem, smem, anywhere],
        out_specs=vmem,
        scratch_shapes=[
            pltpu.VMEM((stored, tw, tw), jnp.bfloat16),
            pltpu.VMEM((stored, tw, tw), jnp.bfloat16),
            [pltpu.VMEM((stored, tw, tw), jnp.bfloat16)] * n_col,
            pltpu.VMEM((n_col, height, kc), jnp.bfloat16),
            pltpu.VMEM((k, breadth), jnp.bfloat16),
            dma((2,)),
            dma((n_row,)),
            dma((n_row, PIECES, 3)),
            dma((n_row, PIECES)),
            dma((n_row, wide + high - 2)),
            dma((n_row, wide - 1, high - 1)),
            dma((n_col, n_row)),
        ],
        compiler_params=pltpu.CompilerParams(
            collective_id=0, has_side_effects=True, vmem_limit_bytes=48 * 2**20
        ),
        cost_estimate=pl.CostEstimate(
            flops=2 * height * breadth * k, bytes_accessed=4 * height * breadth, transcendentals=0
        ),
    )(packed_tiles, source_pick, owner_place, tile_orient, w_panel)
    strips = 3
    return pl.pallas_call(
        antisymmetrize,
        grid=(height // VW, breadth // VW, strips),
        out_shape=jax.ShapeDtypeStruct((height, breadth), jnp.bfloat16),
        in_specs=[vmem],
        out_specs=pl.BlockSpec((VW // strips, VW), lambda i, j, a: (i * strips + a, j)),
        compiler_params=pltpu.CompilerParams(vmem_limit_bytes=16 * 2**20),
        cost_estimate=pl.CostEstimate(
            flops=height * breadth, bytes_accessed=2 * height * breadth, transcendentals=0
        ),
    )(prod)


def solution(mesh):
    in_specs = (
        P("row", None, "col"),
        P("row", None),
        P("row", None),
        P("row", None),
        P("row", "col"),
    )
    return jax.shard_map(
        functools.partial(on_device, mesh.shape["row"], mesh.shape["col"]),
        mesh=mesh, in_specs=in_specs, out_specs=P("row", "col"), check_vma=False,
    )
```

```python
import functools

import jax
import jax.numpy as jnp
from jax import lax
from jax.experimental import pallas as pl
from jax.experimental.pallas import tpu as pltpu
from jax.sharding import PartitionSpec as P

VW = 768
PIECES = 4
MESH = pl.DeviceIdType.MESH


def kernel(
    n_row, n_col, tiles_hbm, pick, place, orient, w_hbm, prod,
    tiles, outgoing, raw, lam, panel,
    load_sem, a_send, p_send, p_recv, l_send, l_fwd, l_recv,
):
    row, col = lax.axis_index("row"), lax.axis_index("col")
    chip, core = row // 2, row % 2
    chips = n_row // 2
    sibling = chip * 2 + 1 - core
    wide = 2
    high = n_col // wide
    hi, lo = col // wide, col % wide

    stored, tw, _ = tiles.shape
    slots = stored // n_row
    depth = panel.shape[0] // n_row
    height, kc = lam.shape[1], lam.shape[2]
    v_tiles = kc // tw
    breadth = panel.shape[1]
    piece = depth // PIECES

    load_tiles = pltpu.make_async_copy(tiles_hbm, tiles, load_sem.at[0])
    load_tiles.start()
    own_rows = pl.ds(pl.multiple_of(row * depth, depth), depth)
    load_w = pltpu.make_async_copy(w_hbm, panel.at[own_rows], load_sem.at[1])
    load_w.start()

    def row_peer(p):
        return lax.rem(row + p, n_row)

    own = (0, 0)
    x_peers = [(0, p) for p in range(1, wide)]
    y_peers = [(p, 0) for p in range(1, high)]
    diagonals = [(m, n) for n in range(1, wide) for m in range(1, high)]

    def col_of(at):
        return lax.rem(hi + at[0], high) * wide + lax.rem(lo + at[1], wide)

    def number(at):
        return at[0] * wide + at[1]

    barrier = pltpu.get_barrier_semaphore()
    for p in range(1, n_row):
        pl.semaphore_signal(barrier, inc=1, device_id=(row_peer(p), col), device_id_type=MESH)
    for c in x_peers + y_peers:
        pl.semaphore_signal(barrier, inc=1, device_id=(row, col_of(c)), device_id_type=MESH)

    load_tiles.wait()

    def choose(t, carry):
        outgoing[t] = tiles[pick[0, t]]
        return carry

    lax.fori_loop(0, stored, choose, 0)
    pl.semaphore_wait(barrier, n_row - 1 + len(x_peers) + len(y_peers))

    def exchange(p):
        to = row_peer(p)
        return pltpu.make_async_remote_copy(
            src_ref=outgoing.at[pl.ds(to * slots, slots)],
            dst_ref=raw[0].at[pl.ds(row * slots, slots)],
            send_sem=a_send.at[p],
            recv_sem=l_recv.at[0, row],
            device_id=(to, col),
            device_id_type=MESH,
        )

    def pass_on(slot, r, way, to):
        rows = pl.ds(pl.multiple_of(slot * depth + r * piece, piece), piece)
        return pltpu.make_async_remote_copy(
            src_ref=panel.at[rows],
            dst_ref=panel.at[rows],
            send_sem=p_send.at[slot, r, way],
            recv_sem=p_recv.at[slot, r],
            device_id=(to, col),
            device_id_type=MESH,
        )

    def spread(block, s, sem, to):
        there = number(((block[0] - to[0]) % high, (block[1] - to[1]) % wide))
        items = pl.ds(s * slots, slots)
        return pltpu.make_async_remote_copy(
            src_ref=raw[number(block)].at[items],
            dst_ref=raw[there].at[items],
            send_sem=sem,
            recv_sem=l_recv.at[there, s],
            device_id=(row, col_of(to)),
            device_id_type=MESH,
        )

    def arrived(block, s):
        spread(block, s, l_send.at[s, 0], own).wait_recv()

    has_left, has_right = chip > 0, chip < chips - 1

    def to_sides(act):
        for r in range(PIECES):
            @pl.when(has_left)
            def _(r=r):
                act(pass_on(row, r, 0, row - 2))

            @pl.when(has_right)
            def _(r=r):
                act(pass_on(row, r, 1, row + 2))

    def chips_at(t, act):
        if t == 0:
            act(chip)
            return

        @pl.when(chip >= t)
        def _():
            act(chip - t)

        @pl.when(chip + t < chips)
        def _():
            act(chip + t)

    def direct(t):
        def act(q):
            for k in range(2):
                s = q * 2 + k
                arrived(own, s)
                for n, c in enumerate(x_peers + y_peers):
                    spread(own, s, l_send.at[s, n], c).start()

        chips_at(t, act)

    def onward(t):
        def act(q):
            for n, c in enumerate(x_peers):
                arrived(c, q * 2)
                for m, d in enumerate(y_peers):
                    spread(c, q * 2, l_fwd.at[q * 2, n, m], d).start()
            for m, c in enumerate(y_peers):
                arrived(c, q * 2 + 1)
                for n, d in enumerate(x_peers):
                    spread(c, q * 2 + 1, l_fwd.at[q * 2 + 1, n, m], d).start()

        chips_at(t, act)

    def panel_step(t, r):
        @pl.when(chip >= t)
        def _():
            slot = row - 2 * t
            pass_on(slot, r, 1, row).wait_recv()

            @pl.when(has_right)
            def _():
                pass_on(slot, r, 1, row + 2).start()

            pass_on(slot, r, 2, sibling).start()

        @pl.when(chip + t < chips)
        def _():
            slot = row + 2 * t
            pass_on(slot, r, 0, row).wait_recv()

            @pl.when(has_left)
            def _():
                pass_on(slot, r, 0, row - 2).start()

            pass_on(slot, r, 2, sibling).start()

    def rest_of_neighbours():
        for s in range(n_row):
            for c in x_peers if s % 2 else y_peers:
                arrived(c, s)

    def rest_of_diagonals():
        for c in diagonals:
            for s in range(n_row):
                arrived(c, s)

    def assemble(block):
        g, items = col_of(block), raw[number(block)]

        def one(u, carry):
            for v in range(v_tiles):
                o = u * v_tiles + v
                code = orient[0, o]
                tile = items[place[0, o]].astype(jnp.float32)
                turned = jnp.where(code % 2 == 1, tile.T, tile)
                turned = jnp.where(code >= 2, -turned, turned)
                lam[g, pl.ds(pl.multiple_of(u * tw, tw), tw), v * tw:(v + 1) * tw] = turned.astype(jnp.bfloat16)
            return carry

        lax.fori_loop(0, height // tw, one, 0)

    for p in [*range(2, n_row - 1), 1, n_row - 1]:
        exchange(p).start()
    load_w.wait()
    to_sides(lambda copy: copy.start())
    for r in range(PIECES):
        pass_on(row, r, 2, sibling).start()

    def keep(t, carry):
        raw[0][row * slots + t] = outgoing[row * slots + t]
        return carry

    lax.fori_loop(0, slots, keep, 0)
    for n, c in enumerate(x_peers + y_peers):
        spread(own, row, l_send.at[row, n], c).start()
    arrived(own, sibling)
    for n, c in enumerate(x_peers + y_peers):
        spread(own, sibling, l_send.at[sibling, n], c).start()
    for t in range(1, chips - 1):
        direct(t)
    panel_step(1, 0)
    direct(chips - 1)
    panel_step(1, 1)
    onward(0)
    for r in range(2, PIECES):
        panel_step(1, r)
        onward(r - 1)
    for t in range(PIECES - 1, chips - 1):
        onward(t)
    assemble(own)
    onward(chips - 1)
    steps = [(t, r) for t in range(2, chips - 1) for r in range(PIECES)]
    for t, r in steps[:-1]:
        panel_step(t, r)
    rest_of_neighbours()
    for c in x_peers + y_peers:
        assemble(c)
    panel_step(*steps[-1])
    rest_of_diagonals()
    for c in diagonals:
        assemble(c)

    strip = VW // 3
    across_n = breadth // VW

    def multiply(q, first):
        for r in range(PIECES):
            pass_on(q * 2 + 1 - core, r, 2, sibling).wait_recv()

        def one(step, carry):
            i, j = step // across_n, step % across_n
            down = pl.ds(pl.multiple_of(i * strip, strip), strip)
            across = pl.ds(pl.multiple_of(j * VW, VW), VW)
            term = jnp.dot(
                lam[q, down, :], panel[pl.ds(pl.multiple_of(q * kc, kc), kc), across],
                preferred_element_type=jnp.float32,
            )
            prod[down, across] = term if first else prod[down, across] + term
            return carry

        lax.fori_loop(0, height // strip * across_n, one, 0)

    multiply(chip, True)
    for t in range(1, chips):
        if t == chips - 1:
            for r in range(PIECES):
                panel_step(t, r)
        chips_at(t, functools.partial(multiply, first=False))

    for p in range(1, n_row):
        exchange(p).wait_send()
    for s in range(n_row):
        for n in range(wide + high - 2):
            spread(own, s, l_send.at[s, n], own).wait_send()
        for n in range(wide - 1):
            for m in range(high - 1):
                spread(own, s, l_fwd.at[s, n, m], own).wait_send()
    to_sides(lambda copy: copy.wait_send())
    for r in range(PIECES):
        pass_on(row, r, 2, sibling).wait_send()
        for t in range(1, chips):
            @pl.when(chip >= t)
            def _(t=t, r=r):
                @pl.when(has_right)
                def _():
                    pass_on(row - 2 * t, r, 1, row + 2).wait_send()

                pass_on(row - 2 * t, r, 2, sibling).wait_send()

            @pl.when(chip + t < chips)
            def _(t=t, r=r):
                @pl.when(has_left)
                def _():
                    pass_on(row + 2 * t, r, 0, row - 2).wait_send()

                pass_on(row + 2 * t, r, 2, sibling).wait_send()


def antisymmetrize(prod, out):
    strip = out.shape[0]
    i, j, a = pl.program_id(0), pl.program_id(1), pl.program_id(2)
    across = pl.ds(pl.multiple_of(j * VW, VW), VW)
    straight = prod[pl.ds(pl.multiple_of(i * VW + a * strip, strip), strip), across]
    crossed = prod[pl.ds(pl.multiple_of(i * VW, VW), VW), pl.ds(pl.multiple_of(j * VW + a * strip, strip), strip)]
    out[...] = (straight - crossed.T).astype(out.dtype)


def on_device(n_row, n_col, packed_tiles, source_pick, owner_place, tile_orient, w_panel):
    stored, tw, _ = packed_tiles.shape
    depth, breadth = w_panel.shape
    k = depth * n_row
    kc = k // n_col
    assert kc == 2 * depth
    height = stored // (kc // tw) * tw
    wide = 2
    high = n_col // wide
    dma = pltpu.SemaphoreType.DMA
    smem = pl.BlockSpec(memory_space=pltpu.SMEM)
    vmem = pl.BlockSpec(memory_space=pltpu.VMEM)
    anywhere = pl.BlockSpec(memory_space=pl.ANY)
    prod = pl.pallas_call(
        functools.partial(kernel, n_row, n_col),
        out_shape=pltpu.VMEM((height, breadth), jnp.float32),
        in_specs=[anywhere, smem, smem, smem, anywhere],
        out_specs=vmem,
        scratch_shapes=[
            pltpu.VMEM((stored, tw, tw), jnp.bfloat16),
            pltpu.VMEM((stored, tw, tw), jnp.bfloat16),
            [pltpu.VMEM((stored, tw, tw), jnp.bfloat16)] * n_col,
            pltpu.VMEM((n_col, height, kc), jnp.bfloat16),
            pltpu.VMEM((k, breadth), jnp.bfloat16),
            dma((2,)),
            dma((n_row,)),
            dma((n_row, PIECES, 3)),
            dma((n_row, PIECES)),
            dma((n_row, wide + high - 2)),
            dma((n_row, wide - 1, high - 1)),
            dma((n_col, n_row)),
        ],
        compiler_params=pltpu.CompilerParams(
            collective_id=0, has_side_effects=True, vmem_limit_bytes=48 * 2**20
        ),
        cost_estimate=pl.CostEstimate(
            flops=2 * height * breadth * k, bytes_accessed=4 * height * breadth, transcendentals=0
        ),
    )(packed_tiles, source_pick, owner_place, tile_orient, w_panel)
    strips = 1
    return pl.pallas_call(
        antisymmetrize,
        grid=(height // VW, breadth // VW, strips),
        out_shape=jax.ShapeDtypeStruct((height, breadth), jnp.bfloat16),
        in_specs=[vmem],
        out_specs=pl.BlockSpec((VW // strips, VW), lambda i, j, a: (i * strips + a, j)),
        compiler_params=pltpu.CompilerParams(vmem_limit_bytes=16 * 2**20),
        cost_estimate=pl.CostEstimate(
            flops=height * breadth, bytes_accessed=2 * height * breadth, transcendentals=0
        ),
    )(prod)


def solution(mesh):
    in_specs = (
        P("row", None, "col"),
        P("row", None),
        P("row", None),
        P("row", None),
        P("row", "col"),
    )
    return jax.shard_map(
        functools.partial(on_device, mesh.shape["row"], mesh.shape["col"]),
        mesh=mesh, in_specs=in_specs, out_specs=P("row", "col"), check_vma=False,
    )
```
